32 devices in a mesh: inp: 4 (over x, core), chan: 8 (over z, y).
Axes of the slice: x: 2, y: 2, z: 4, core: 2. Of those that a mesh axis runs over, the one named last changes fastest.
Arguments:
- voltages: bfloat16 [1024, 262144], P('inp', 'chan'), may hold values from -4 to 4
- scale_codes: int32 [1024], P('inp'), may hold values from 4 to 32
- kept_channels: int32 [128], replicated, may hold values from 0 to 4095, as said below
Outputs:
- visibilities: float32 [2, 128, 1024, 1024], P(None, 'chan', 'inp')
The draws below stay inside these ranges and needn't reach their ends.
Inputs may be any that keep to these rules, and one draw needn't show every extreme that they name: `kept_channels`: 128 distinct channel numbers.
All inputs are finite; a program needn't handle non-finite values.
Results may differ from the reference program's by a relative error of at most 0.0036.
Values may be sent and summed in bfloat16 or wider, within the bound.
No kernel may reach another device: no remote copies, remote signals or barrier semaphores. Data moves between devices by JAX's collectives and lax.ppermute only.
A program may use at most 384 MiB of HBM per device.

```python
import jax
import jax.numpy as jnp
from jax import lax

INPUTS = 1024
TRANSFORM = 8192
CHANNELS = 4096
KEPT = 128
TAPS = 4
SPECTRA = 32
SAMPLES = 262144


def draw_kept_channels(key, part):
    middle = jax.random.permutation(key, CHANNELS - 2)[:KEPT - 2].astype(jnp.int32) + 1
    whole = jnp.concatenate([jnp.zeros((1,), jnp.int32), middle, jnp.full((1,), CHANNELS - 1, jnp.int32)])
    order = jax.random.permutation(jax.random.fold_in(key, 7), KEPT)
    return whole[order].astype(jnp.int32)


def plant(entries, stream_key, smallest, top_value):
    longest = entries.shape.index(max(entries.shape))
    spots = []
    for shift in (0, 1):
        where = [jax.random.randint(jax.random.fold_in(stream_key, axis), (), 0, length) for axis, length in enumerate(entries.shape)]
        where[longest] = (where[longest] + shift) % entries.shape[longest]
        spots.append(tuple(where))
    return entries.at[spots[0]].set(smallest).at[spots[1]].set(top_value)


def levels(rng, extent, cuts, smallest, top_value):
    loudness = 1.0
    for dim, parts in cuts:
        steps = jax.random.uniform(jax.random.fold_in(jax.random.fold_in(rng, 6), dim), (parts,), jnp.float32, smallest / len(cuts), top_value / len(cuts))
        loudness = loudness * jnp.repeat(jnp.exp(steps), extent[dim] // parts).reshape((-1,) + (1,) * (len(extent) - 1 - dim))
    return loudness


def gaussian(own_key, shape, width, limit, split=(), held_as=jnp.bfloat16):
    array = jax.random.normal(own_key, shape, jnp.float32) * width
    if len(split) > 0:
        array = levels(own_key, shape, split, -0.22, 0.18) * array
    return jnp.clip(array, min=-limit, max=limit).astype(held_as)


def setup_inputs(seed: int = 0) -> dict:
    key_list = jax.random.split(jax.random.key(seed), 4)
    return {
        "voltages": gaussian(key_list[0], (INPUTS, SAMPLES), 1.0, 4.0, ((0, 4), (1, 8))),
        "scale_codes": plant(jax.random.randint(key_list[1], (INPUTS,), 4, 33), jax.random.fold_in(key_list[1], 1), 4, 32).astype(jnp.int32),
        "kept_channels": draw_kept_channels(jax.random.fold_in(key_list[3], 71), 0),
    }


def prototype():
    sample = jnp.arange(TAPS * TRANSFORM, dtype=jnp.float32)
    offset = (sample + 0.5) / TRANSFORM - TAPS / 2.0
    window = 0.5 - 0.5 * jnp.cos(2.0 * jnp.pi * (sample + 0.5) / (TAPS * TRANSFORM))
    return (jnp.sinc(offset) * window).reshape(TAPS, TRANSFORM)

def reference(voltages, scale_codes, kept_channels):
    coeffs = prototype()
    groups = voltages.reshape(INPUTS // 32, 32, SPECTRA, TRANSFORM)
    code_groups = scale_codes.reshape(INPUTS // 32, 32)

    def channelize(operands):
        group_in, code_group = operands
        samples = group_in.astype(jnp.float32)
        padded = jnp.pad(samples, ((0, 0), (TAPS - 1, 0), (0, 0)))
        filtered = sum((coeffs[tap_index] * padded[:, tap_index:tap_index + SPECTRA] for tap_index in range(TAPS)))
        spectrum = jnp.fft.rfft(filtered, axis=-1)[..., kept_channels] / jnp.sqrt(jnp.float32(TRANSFORM))
        stacked = jnp.stack([jnp.real(spectrum), jnp.imag(spectrum)], axis=-1)
        scales = code_group.astype(jnp.float32) / 16.0
        return (stacked * scales[:, None, None, None]).astype(jnp.bfloat16)
    channelized = lax.map(channelize, (groups, code_groups)).reshape(INPUTS, SPECTRA, KEPT, 2)

    def correlate(channel):
        column = lax.dynamic_index_in_dim(channelized, channel, axis=2, keepdims=False)
        rows = column.reshape(INPUTS, 2 * SPECTRA)
        rotated = jnp.stack([-column[..., 1], column[..., 0]], axis=-1).reshape(INPUTS, 2 * SPECTRA)
        real_part = jnp.dot(rows, rows.T, preferred_element_type=jnp.float32)
        imag_part = jnp.dot(rows, rotated.T, preferred_element_type=jnp.float32)
        return jnp.stack([real_part, imag_part]) / SPECTRA
    result = lax.map(correlate, jnp.arange(KEPT, dtype=jnp.int32))
    return jnp.moveaxis(result, 1, 0)
```

```python
import functools

import jax
import jax.numpy as jnp
from jax import lax
from jax.experimental import pallas as pl
from jax.experimental.pallas import tpu as pltpu
from jax.sharding import PartitionSpec as P

TRANSFORM = 8192
TAPS = 4
SUB = 128
LANES = 128
DEPTH = 1024
VMEM = 60 * 1024 * 1024


def prototype():
    sample = jnp.arange(TAPS * TRANSFORM, dtype=jnp.float32)
    offset = (sample + 0.5) / TRANSFORM - TAPS / 2.0
    window = 0.5 - 0.5 * jnp.cos(2.0 * jnp.pi * (sample + 0.5) / (TAPS * TRANSFORM))
    return (jnp.sinc(offset) * window).reshape(TAPS, TRANSFORM)


def angle_tables(kept_channels):
    coarse = jnp.arange(TRANSFORM // SUB, dtype=jnp.int32) * SUB
    fine = jnp.arange(SUB, dtype=jnp.int32)
    sample = jnp.concatenate([coarse, fine])
    turns = kept_channels[None, :] * sample[:, None] % TRANSFORM
    quarter = jnp.where(jnp.arange(sample.shape[0]) < coarse.shape[0], 0, TRANSFORM // 4)
    turns = jnp.concatenate([turns, (turns + quarter[:, None]) % TRANSFORM], axis=1)
    angles = turns.astype(jnp.float32) * (2.0 * jnp.pi / TRANSFORM)
    norming = jnp.where(quarter == 0, 1.0 / jnp.sqrt(jnp.float32(TRANSFORM)), 1.0)[:, None]
    return jnp.cos(angles) * norming, jnp.sin(angles) * norming


def dft_kernel(planes, frames, groups, *refs):
    nf = len(frames)
    samples = dict(zip(frames, refs[:nf]))
    coeff, cos_a, sin_a, cos_b, sin_b, scale = refs[nf : nf + 6]
    outs = refs[nf + 6 : nf + 6 + len(groups)]
    acc = refs[-1]
    step = pl.program_id(0)

    @pl.when(step == 0)
    def _():
        acc[...] = jnp.zeros_like(acc)

    cb, sb = cos_b[...], sin_b[...]
    table = jnp.concatenate(
        [cos_a[r : r + 1, :] * cb - sin_a[r : r + 1, :] * sb for r in range(DEPTH // SUB)], axis=0
    )
    t_hi = table.astype(jnp.bfloat16)
    t_lo = (table - t_hi.astype(jnp.float32)).astype(jnp.bfloat16)
    dot = functools.partial(jnp.dot, preferred_element_type=jnp.float32)
    volts = {f: samples[f][...].astype(jnp.float32) for f in frames}
    for p, (s, passes) in enumerate(planes):
        x = None
        for t in range(TAPS):
            f = s - (TAPS - 1) + t
            if f in volts:
                term = coeff[t : t + 1, :] * volts[f]
                x = term if x is None else x + term
        hi = x.astype(jnp.bfloat16)
        total = dot(hi, t_hi)
        if passes > 1:
            total += dot(hi, t_lo)
        if passes > 2:
            total += dot((x - hi.astype(jnp.float32)).astype(jnp.bfloat16), t_hi)
        acc[p] += total

    @pl.when(step == pl.num_programs(0) - 1)
    def _():
        for out, (members, dtype) in zip(outs, groups):
            for i, p in enumerate(members):
                out[i] = (acc[p].T * scale[...]).astype(dtype)


def spectra(voltages, coeffs, tables, scales, planes, groups):
    rows = voltages.shape[0]
    own = voltages.shape[1] // TRANSFORM
    steps = TRANSFORM // DEPTH
    columns = tables[0].shape[1]
    coarse = TRANSFORM // SUB
    frames = sorted({s - (TAPS - 1) + t for s, _ in planes for t in range(TAPS)} & set(range(own)))
    per_step = DEPTH // SUB

    def frame_spec(f):
        return pl.BlockSpec((rows, DEPTH), lambda j: (0, f * steps + j))

    coarse_spec = pl.BlockSpec((per_step, columns), lambda j: (j, 0))
    fine_spec = pl.BlockSpec((SUB, columns), lambda j: (0, 0))
    cos_t, sin_t = tables
    outs = [jax.ShapeDtypeStruct((len(m), columns, rows), d) for m, d in groups]
    flops = 2 * rows * TRANSFORM * columns * sum(p for _, p in planes)
    return pl.pallas_call(
        functools.partial(dft_kernel, planes, frames, groups),
        grid=(steps,),
        in_specs=[frame_spec(f) for f in frames]
        + [pl.BlockSpec((TAPS, DEPTH), lambda j: (0, j))]
        + [coarse_spec, coarse_spec, fine_spec, fine_spec]
        + [pl.BlockSpec((1, rows), lambda j: (0, 0))],
        out_specs=[pl.BlockSpec(o.shape, lambda j: (0, 0, 0)) for o in outs],
        out_shape=outs,
        scratch_shapes=[pltpu.VMEM((len(planes), rows, columns), jnp.float32)],
        compiler_params=pltpu.CompilerParams(vmem_limit_bytes=VMEM),
        cost_estimate=pl.CostEstimate(
            flops=flops, bytes_accessed=len(frames) * rows * TRANSFORM * 2, transcendentals=0
        ),
    )(*[voltages] * len(frames), coeffs, cos_t[:coarse], sin_t[:coarse], cos_t[coarse:], sin_t[coarse:], scales)


def combine_kernel(parts, place, own, ahead, behind, *refs):
    outs, mixed = refs[:-1], refs[-1]
    me = place[0]
    slots, columns = own.shape[0], own.shape[1]
    kept = columns // 2
    inside = jnp.where(me == parts - 1, 0.0, 1.0)
    back = behind.shape[0]
    for s in range(slots):
        value = own[s]
        if s == 0:
            value = value + ahead[0].astype(jnp.float32)
        if s >= slots - back:
            value = value * inside + behind[s - (slots - back)].astype(jnp.float32)
        for p in range(2):
            for h in range(mixed.shape[0]):
                mixed[h, pl.ds(p * slots + s, kept, stride=2 * slots), :] = value[
                    p * kept : (p + 1) * kept, h * LANES : (h + 1) * LANES
                ]
    rows = outs[0].shape[0]
    for d, out in enumerate(outs):
        start = pl.multiple_of(jnp.bitwise_xor(me, d) * rows, rows)
        for h in range(mixed.shape[0]):
            out[:, h * LANES : (h + 1) * LANES] = mixed[h, pl.ds(start, rows), :].astype(out.dtype)


def combined(parts, me, own, ahead, behind):
    slots, columns, rows = own.shape
    block = columns * slots // parts
    whole = pl.BlockSpec(memory_space=pltpu.VMEM)
    return pl.pallas_call(
        functools.partial(combine_kernel, parts),
        in_specs=[pl.BlockSpec(memory_space=pltpu.SMEM)] + [whole] * 3,
        out_specs=[whole] * parts,
        out_shape=[jax.ShapeDtypeStruct((block, rows), jnp.bfloat16)] * parts,
        scratch_shapes=[pltpu.VMEM((rows // LANES, slots * columns, LANES), jnp.float32)],
        compiler_params=pltpu.CompilerParams(vmem_limit_bytes=VMEM),
    )(me, own, ahead, behind)


def correlate_kernel(parts, half, spectra_count, place, *refs):
    mine, theirs, out = refs[:parts], refs[parts : 2 * parts], refs[-1]
    wide = 2 * half
    for c in range(mine[0].shape[0] // wide):
        take = slice(c * wide, (c + 1) * wide)
        left = jnp.concatenate([m[take].astype(jnp.float32) for m in mine], axis=0)
        right = jnp.concatenate([m[take].astype(jnp.float32) for m in theirs], axis=0).astype(jnp.bfloat16)
        count = left.shape[0]
        row = lax.broadcasted_iota(jnp.int32, left.shape, 0) % wide
        turned = jnp.where(row < half, pltpu.roll(left, count - half, 0), -pltpu.roll(left, half, 0))
        both = jnp.concatenate([left.T, turned.T], axis=0).astype(jnp.bfloat16)
        result = jnp.dot(both, right, preferred_element_type=jnp.float32) * (1.0 / spectra_count)
        out[0, c] = result[: left.shape[1]]
        out[1, c] = result[left.shape[1] :]


def correlated(column, mine, theirs, half, spectra_count, total, before=None):
    parts = len(mine)
    block, rows = mine[0].shape
    wide = 2 * half
    pair = max(1, 16 // wide)
    steps = block // (pair * wide)
    shape = jax.ShapeDtypeStruct((2, block // wide, rows, total), jnp.float32)
    spec = pl.BlockSpec((pair * wide, rows), lambda j, place: (j, 0))
    operands = [column, *mine, *theirs]
    in_specs = [spec] * (2 * parts)
    aliases = {}
    if before is not None:
        operands.append(before)
        in_specs.append(pl.BlockSpec(memory_space=pl.ANY))
        aliases = {len(operands) - 1: 0}
    return pl.pallas_call(
        functools.partial(correlate_kernel, parts, half, spectra_count),
        grid_spec=pltpu.PrefetchScalarGridSpec(
            num_scalar_prefetch=1,
            grid=(steps,),
            in_specs=in_specs,
            out_specs=pl.BlockSpec((2, pair, rows, rows), lambda j, place: (0, j, 0, place[0])),
        ),
        out_shape=shape,
        input_output_aliases=aliases,
        compiler_params=pltpu.CompilerParams(vmem_limit_bytes=VMEM),
        cost_estimate=pl.CostEstimate(
            flops=4 * spectra_count * 2 * rows * rows * 2 * block // wide,
            bytes_accessed=2 * block // wide * rows * rows * 4,
            transcendentals=0,
        ),
    )(*operands)


def exchanged(block, axis, mask):
    return lax.ppermute(block, axis, [(i, i ^ mask) for i in range(lax.axis_size(axis))])


def local(voltages, scale_codes, kept_channels):
    rows = voltages.shape[0]
    own = voltages.shape[1] // TRANSFORM
    history = TAPS - 1
    parts, groups = lax.axis_size("chan"), lax.axis_size("inp")
    me, seat = lax.axis_index("chan"), lax.axis_index("inp")
    coeffs = prototype()
    tables = angle_tables(kept_channels)
    scales = (scale_codes.astype(jnp.float32) / 16.0)[None, :]
    first = 2
    last = first + own
    edge = [(s, 1 if s in (0, own + history - 1) else 2) for s in [*range(first), *range(last, own + history)]]
    inner = [(s, 2 if s == last - 1 else 3) for s in range(first, last)]
    behind, ahead = spectra(
        voltages, coeffs, tables, scales, edge,
        [(list(range(first)), jnp.bfloat16), (list(range(first, len(edge))), jnp.bfloat16)],
    )
    ahead = lax.ppermute(ahead, "chan", [(i, i + 1) for i in range(parts - 1)])
    behind = lax.ppermute(behind, "chan", [(i, (i - 1) % parts) for i in range(parts)])
    (planes,) = spectra(voltages, coeffs, tables, scales, inner, [(list(range(own)), jnp.float32)])
    blocks = combined(parts, me[None], planes, ahead, behind)
    keep, near = blocks[0::2], [exchanged(b, "chan", 1) for b in blocks[1::2]]
    mine = [keep[0], near[0]]
    for i in range(1, parts // 2):
        mine += [exchanged(keep[i], "chan", 2 * i), exchanged(near[i], "chan", 2 * i)]
    spectra_count = own * parts
    total = rows * groups
    half = own
    across = [exchanged(m, "inp", 2) for m in mine]
    beside = [exchanged(m, "inp", 1) for m in mine]
    corner = [exchanged(m, "inp", 1) for m in across]
    result = None
    for mask, theirs in ((0, mine), (1, beside), (2, across), (3, corner)):
        column = jnp.bitwise_xor(seat, mask)[None].astype(jnp.int32)
        result = correlated(column, mine, theirs, half, spectra_count, total, result)
    return result


def solution(mesh):
    placed = (P("inp", "chan"), P("inp"), P())
    return jax.shard_map(
        local, mesh=mesh, in_specs=placed, out_specs=P(None, "chan", "inp", None), check_vma=False
    )
```

```python
import functools

import jax
import jax.numpy as jnp
import numpy as np
from jax import lax
from jax.experimental import pallas as pl
from jax.experimental.pallas import tpu as pltpu
from jax.sharding import PartitionSpec as P

TRANSFORM = 8192
TAPS = 4
LANES = 128
SUB = 128
DEPTH = 512
PER_STEP = 2
CHUNK = 16
VMEM = 60 * 1024 * 1024
PIECES = 2


def prototype():
    sample = np.arange(TAPS * TRANSFORM, dtype=np.float64).reshape(TAPS, TRANSFORM)[:, : TRANSFORM // 2]
    offset = (sample + 0.5) / TRANSFORM - TAPS / 2.0
    window = 0.5 - 0.5 * np.cos(2.0 * np.pi * (sample + 0.5) / (TAPS * TRANSFORM))
    return (np.sinc(offset) * window).astype(np.float32)


def angle_tables(kept_channels):
    circle = 2 * TRANSFORM
    row = jnp.arange(SUB + TRANSFORM // 2 // SUB, dtype=jnp.int32)
    twice = jnp.where(row < SUB, 2 * row + 1, 2 * SUB * (row - SUB))[:, None]
    angles = (kept_channels[None, :] * twice % circle).astype(jnp.float32) * (2.0 * jnp.pi / circle)
    return jnp.cos(angles), jnp.sin(angles)


def dft_kernel(planes, frames, groups, *refs):
    nf, ng = len(frames), len(groups)
    ahead, mirror = refs[:nf], refs[nf : 2 * nf]
    coeff, cos_c, sin_c, cos_f, sin_f, codes = refs[2 * nf : 2 * nf + 6]
    outs, refs = refs[2 * nf + 6 : 2 * nf + 6 + ng], refs[2 * nf + 6 + ng :]
    acc_even, acc_odd = refs[:2]
    rows = ahead[0].shape[0]
    kept = cos_f.shape[1]
    step = pl.program_id(0)
    low = [p for p, (_, wanted) in enumerate(planes) if wanted]
    place = {p: (len(planes) + i) * rows for i, p in enumerate(low)}
    width = 2 * LANES
    span = DEPTH * PER_STEP
    backwards = LANES - 1 - lax.broadcasted_iota(jnp.int32, (CHUNK, LANES), 1)

    @pl.when(step == 0)
    def _():
        acc_even[...] = jnp.zeros_like(acc_even)
        acc_odd[...] = jnp.zeros_like(acc_odd)

    for u in range(PER_STEP):
        even, odd, t_even, t_odd = refs[2 + 4 * u : 6 + 4 * u]
        for b in range(DEPTH // SUB):
            block = u * (DEPTH // SUB) + b
            for q in range(0, SUB, CHUNK):
                here = slice(b * SUB + q, b * SUB + q + CHUNK)
                cos_b, sin_b = cos_c[block : block + 1, :], sin_c[block : block + 1, :]
                cos_q, sin_q = cos_f[q : q + CHUNK, :], sin_f[q : q + CHUNK, :]
                for held, table in (
                    (t_even, cos_b * cos_q - sin_b * sin_q),
                    (t_odd, sin_b * cos_q + cos_b * sin_q),
                ):
                    high = table.astype(jnp.bfloat16)
                    held[here, :kept] = high
                    held[here, kept:] = (table - high.astype(jnp.float32)).astype(jnp.bfloat16)
        for w in range(0, DEPTH, width):
            at = u * DEPTH + w
            taps = [jnp.broadcast_to(coeff[t : t + 1, at : at + width], (CHUNK, width)) for t in range(TAPS)]
            for r in range(0, rows, CHUNK):
                fore, rear = {}, {}
                for i, f in enumerate(frames):
                    fore[f] = ahead[i][r : r + CHUNK, at : at + width].astype(jnp.float32)
                    seen = mirror[i][r : r + CHUNK, span - at - width : span - at].astype(jnp.float32)
                    rear[f] = jnp.concatenate(
                        [
                            jnp.take_along_axis(seen[:, c : c + LANES], backwards, axis=1)
                            for c in range(width - LANES, -1, -LANES)
                        ],
                        axis=1,
                    )
                for p, (s, _) in enumerate(planes):
                    x = z = None
                    for t in range(TAPS):
                        f = s - (TAPS - 1) + t
                        if f in fore:
                            a, b = taps[t] * fore[f], taps[TAPS - 1 - t] * rear[f]
                            x, z = (a, b) if x is None else (x + a, z + b)
                    for value, held in ((x + z, even), (x - z, odd)):
                        high = value.astype(jnp.bfloat16)
                        held[p * rows + r : p * rows + r + CHUNK, w : w + width] = high
                        if p in place:
                            rest = (value - high.astype(jnp.float32)).astype(jnp.bfloat16)
                            held[place[p] + r : place[p] + r + CHUNK, w : w + width] = rest
        acc_even[...] += jnp.dot(even[...], t_even[...], preferred_element_type=jnp.float32)
        acc_odd[...] += jnp.dot(odd[...], t_odd[...], preferred_element_type=jnp.float32)

    @pl.when(step == pl.num_programs(0) - 1)
    def _():
        def total(acc, p):
            value = acc[p * rows : (p + 1) * rows, :kept] + acc[p * rows : (p + 1) * rows, kept:]
            if p in place:
                rest = slice(place[p], place[p] + rows)
                value = value + acc[rest, :kept] + acc[rest, kept:]
            return value

        cos_h, sin_h = cos_f[0:1, :], sin_f[0:1, :]
        scale = codes[...].astype(jnp.float32) * (TRANSFORM**-0.5 / 16.0)
        for out, (members, dtype) in zip(outs, groups):
            for i, p in enumerate(members):
                even, odd = total(acc_even, p), total(acc_odd, p)
                out[i, :kept] = ((cos_h * even + sin_h * odd).T * scale).astype(dtype)
                out[i, kept:] = ((sin_h * even - cos_h * odd).T * scale).astype(dtype)


def spectra(voltages, coeffs, tables, codes, planes, groups, piece=0, pieces=1):
    rows = voltages.shape[0] // pieces
    own = voltages.shape[1] // TRANSFORM
    span = DEPTH * PER_STEP
    steps = TRANSFORM // 2 // span
    kept = tables[0].shape[1]
    columns = 2 * kept
    frames = sorted({s - (TAPS - 1) + t for s, _ in planes for t in range(TAPS)} & set(range(own)))
    count = len(planes) + sum(wanted for _, wanted in planes)

    def ahead(f):
        return pl.BlockSpec((rows, span), lambda j: (piece, 2 * f * steps + j))

    def mirror(f):
        return pl.BlockSpec((rows, span), lambda j: (piece, 2 * f * steps + 2 * steps - 1 - j))

    coarse = pl.BlockSpec((span // SUB, kept), lambda j: (SUB // (span // SUB) + j, 0))
    fine = pl.BlockSpec((SUB, kept), lambda j: (0, 0))
    cos_t, sin_t = tables
    outs = [jax.ShapeDtypeStruct((len(m), columns, rows), d) for m, d in groups]
    part = [
        pltpu.VMEM((count * rows, DEPTH), jnp.bfloat16),
        pltpu.VMEM((count * rows, DEPTH), jnp.bfloat16),
        pltpu.VMEM((DEPTH, columns), jnp.bfloat16),
        pltpu.VMEM((DEPTH, columns), jnp.bfloat16),
    ]
    return pl.pallas_call(
        functools.partial(dft_kernel, planes, frames, groups),
        grid=(steps,),
        in_specs=[ahead(f) for f in frames]
        + [mirror(f) for f in frames]
        + [pl.BlockSpec((TAPS, span), lambda j: (0, j)), coarse, coarse, fine, fine]
        + [pl.BlockSpec((1, rows), lambda j: (0, piece))],
        out_specs=[pl.BlockSpec(o.shape, lambda j: (0, 0, 0)) for o in outs],
        out_shape=outs,
        scratch_shapes=[pltpu.VMEM((count * rows, columns), jnp.float32)] * 2 + part * PER_STEP,
        compiler_params=pltpu.CompilerParams(vmem_limit_bytes=VMEM),
        cost_estimate=pl.CostEstimate(
            flops=2 * rows * TRANSFORM * columns * count,
            bytes_accessed=len(frames) * rows * TRANSFORM * 2,
            transcendentals=0,
        ),
    )(*[voltages] * (2 * len(frames)), coeffs, cos_t, sin_t, cos_t, sin_t, codes)


def combine_kernel(parts, place, own, ahead, behind, out, mixed):
    me = place[0]
    slots, columns = own.shape[0], own.shape[1]
    kept = columns // 2
    inside = jnp.where(me == parts - 1, 0.0, 1.0)
    back = behind.shape[0]
    for s in range(slots):
        value = own[s]
        if s == 0:
            value = value + ahead[0].astype(jnp.float32)
        if s >= slots - back:
            value = value * inside + behind[s - (slots - back)].astype(jnp.float32)
        for p in range(2):
            for h in range(mixed.shape[0]):
                mixed[h, pl.ds(p * slots + s, kept, stride=2 * slots), :] = value[
                    p * kept : (p + 1) * kept, h * LANES : (h + 1) * LANES
                ]
    for h in range(mixed.shape[0]):
        for i in range(out.shape[0]):
            rows = out.shape[1]
            out[i, :, h * LANES : (h + 1) * LANES] = mixed[h, i * rows : (i + 1) * rows, :].astype(out.dtype)


def combined(parts, me, own, ahead, behind, piece):
    slots, columns, rows = own.shape
    block = columns * slots // parts

    def arriving(x):
        return pl.BlockSpec((x.shape[0], columns, rows), lambda j: (0, 0, piece))

    return pl.pallas_call(
        functools.partial(combine_kernel, parts),
        grid=(1,),
        in_specs=[pl.BlockSpec(memory_space=pltpu.SMEM), pl.BlockSpec(own.shape, lambda j: (0, 0, 0))]
        + [arriving(ahead), arriving(behind)],
        out_specs=pl.BlockSpec((parts, block, rows), lambda j: (0, 0, 0)),
        out_shape=jax.ShapeDtypeStruct((parts, block, rows), jnp.bfloat16),
        scratch_shapes=[pltpu.VMEM((rows // LANES, slots * columns, LANES), jnp.float32)],
        compiler_params=pltpu.CompilerParams(vmem_limit_bytes=VMEM),
    )(me, own, ahead, behind)


def correlate_kernel(half, pair, spectra_count, pieces, sets, groups, seat, *refs):
    out = refs[-1]
    wide = 2 * half
    step = pl.program_id(0)
    tile = 16 // wide
    me = seat[0]

    def gathered(tiles, take):
        return jnp.concatenate([jnp.concatenate([t[take] for t in p], axis=0) for p in tiles], axis=1)

    for group in range(pair // tile):
        at = pl.multiple_of((step * pair + group * tile) * wide, 16)
        tiles = [
            [
                [
                    refs[(m * pieces + p) * sets + k][i, pl.ds(at, 16), :].astype(jnp.float32)
                    for k in range(sets)
                    for i in range(refs[k].shape[0])
                ]
                for p in range(pieces)
            ]
            for m in range(groups)
        ]
        for h in range(tile):
            c = group * tile + h
            columns = [gathered(t, slice(h * wide, (h + 1) * wide)) for t in tiles]
            left = columns[0]
            bit = 1
            while bit < groups:
                swap = (me // bit) % 2 == 1
                columns = [jnp.where(swap, columns[q ^ bit], columns[q]) for q in range(groups)]
                bit *= 2
            right = jnp.concatenate(columns, axis=1).astype(jnp.bfloat16)
            row = lax.broadcasted_iota(jnp.int32, left.shape, 0) % wide
            turned = jnp.where(row < half, pltpu.roll(left, left.shape[0] - half, 0), -pltpu.roll(left, half, 0))
            both = jnp.concatenate([left.T, turned.T], axis=0).astype(jnp.bfloat16)
            result = jnp.dot(both, right, preferred_element_type=jnp.float32) * (1.0 / spectra_count)
            out[0, c], out[1, c] = result[: left.shape[1]], result[left.shape[1] :]


def correlated(seat, seen, half, spectra_count):
    groups, pieces, sets = len(seen), len(seen[0]), len(seen[0][0])
    wide = 2 * half
    block = seen[0][0][0].shape[1]
    rows = sum(p[0].shape[2] for p in seen[0])
    channels = block // wide
    pair = min(channels, 16 // wide)
    arrays = [a for mask in seen for piece in mask for a in piece]
    return pl.pallas_call(
        functools.partial(correlate_kernel, half, pair, spectra_count, pieces, sets, groups),
        grid_spec=pltpu.PrefetchScalarGridSpec(
            num_scalar_prefetch=1,
            grid=(channels // pair,),
            in_specs=[pl.BlockSpec(a.shape, lambda j, seat: (0, 0, 0)) for a in arrays],
            out_specs=pl.BlockSpec((2, pair, rows, groups * rows), lambda j, seat: (0, j, 0, 0)),
        ),
        out_shape=jax.ShapeDtypeStruct((2, channels, rows, groups * rows), jnp.float32),
        compiler_params=pltpu.CompilerParams(vmem_limit_bytes=VMEM),
        cost_estimate=pl.CostEstimate(
            flops=8 * spectra_count * rows * groups * rows * channels,
            bytes_accessed=2 * channels * rows * groups * rows * 4,
            transcendentals=0,
        ),
    )(seat, *arrays)


def exchanged(block, axis, mask):
    return lax.ppermute(block, axis, [(i, i ^ mask) for i in range(lax.axis_size(axis))])


def local(voltages, scale_codes, kept_channels):
    rows = voltages.shape[0]
    own = voltages.shape[1] // TRANSFORM
    history = TAPS - 1
    parts, groups = lax.axis_size("chan"), lax.axis_size("inp")
    me, seat = lax.axis_index("chan"), lax.axis_index("inp")
    coeffs = prototype()
    tables = angle_tables(kept_channels)
    codes = scale_codes[None, :]
    first = 2
    last = first + own
    edge = [(s, False) for s in [*range(first), *range(last, own + history)]]
    inner = [(s, s < last - 1) for s in range(first, last)]
    behind, ahead = spectra(
        voltages, coeffs, tables, codes, edge,
        [(list(range(first)), jnp.bfloat16), (list(range(first, len(edge))), jnp.bfloat16)],
    )
    ahead = lax.ppermute(ahead, "chan", [(i, i + 1) for i in range(parts - 1)])
    behind = lax.ppermute(behind, "chan", [(i, (i - 1) % parts) for i in range(parts)])
    me, seat = me.astype(jnp.int32).reshape(1), seat.astype(jnp.int32).reshape(1)
    mine = []
    for piece in range(PIECES):
        (planes,) = spectra(voltages, coeffs, tables, codes, inner, [(list(range(own)), jnp.float32)], piece, PIECES)
        blocks = combined(parts, me, planes, ahead, behind, piece)
        mine.append([lax.all_to_all(blocks, "chan", 0, 0, tiled=True)])
    seen = {0: mine}
    bit = groups // 2
    while bit:
        seen.update({m | bit: [[exchanged(b, "inp", bit) for b in p] for p in seen[m]] for m in list(seen)})
        bit //= 2
    return correlated(seat, [seen[m] for m in range(groups)], own, own * parts)


def solution(mesh):
    placed = (P("inp", "chan"), P("inp"), P())
    return jax.shard_map(
        local, mesh=mesh, in_specs=placed, out_specs=P(None, "chan", "inp", None), check_vma=False
    )
```

```python
import functools

import jax
import jax.numpy as jnp
import numpy as np
from jax import lax
from jax.experimental import pallas as pl
from jax.experimental.pallas import tpu as pltpu
from jax.sharding import PartitionSpec as P

TRANSFORM = 8192
TAPS = 4
LANES = 128
SUB = 128
DEPTH = 512
PER_STEP = 2
CHUNK = 16
EDGE_DEPTH = 1024
EDGE_STEPS = 2
VMEM = 60 * 1024 * 1024
PIECES = 2


def prototype():
    sample = np.arange(TAPS * TRANSFORM, dtype=np.float64).reshape(TAPS, TRANSFORM)
    offset = (sample + 0.5) / TRANSFORM - TAPS / 2.0
    window = 0.5 - 0.5 * np.cos(2.0 * np.pi * (sample + 0.5) / (TAPS * TRANSFORM))
    return (np.sinc(offset) * window).astype(np.float32)


def fill_angles(kept, cos_held, sin_held, half=1):
    circle = 2 * TRANSFORM
    row = lax.broadcasted_iota(jnp.int32, cos_held.shape, 0)
    twice = jnp.where(row < SUB, 2 * row + half, 2 * SUB * (row - SUB))
    turns = jnp.bitwise_and(kept[...] * twice, circle - 1)
    angles = turns.astype(jnp.float32) * (2.0 * np.pi / circle)
    cos_held[...] = jnp.cos(angles)
    sin_held[...] = jnp.sin(angles)


def mix(spectra, parts, place, ahead, behind, out, mixed):
    slots, kept = len(spectra), spectra[0][0].shape[0]
    inside = jnp.where(place[0] == parts - 1, 0.0, 1.0)
    back = behind.shape[0]
    for s, values in enumerate(spectra):
        for p, value in enumerate(values):
            here = slice(p * kept, (p + 1) * kept)
            if s == 0:
                value = value + ahead[0, here].astype(jnp.float32)
            if s >= slots - back:
                value = value * inside + behind[s - (slots - back), here].astype(jnp.float32)
            for h in range(mixed.shape[0]):
                mixed[h, pl.ds(p * slots + s, kept, stride=2 * slots), :] = value[:, h * LANES : (h + 1) * LANES]
    rows = out.shape[1]
    for h in range(mixed.shape[0]):
        for i in range(out.shape[0]):
            out[i, :, h * LANES : (h + 1) * LANES] = mixed[h, i * rows : (i + 1) * rows, :].astype(out.dtype)


def dft_kernel(planes, frames, groups, extra, parts, *refs):
    nf, ng = len(frames), len(groups)
    ahead, mirror = refs[:nf], refs[nf : 2 * nf]
    coeff, channels, codes = refs[2 * nf : 2 * nf + 3]
    arrived, refs = refs[2 * nf + 3 : 2 * nf + 3 + extra], refs[2 * nf + 3 + extra :]
    outs, refs = refs[:ng], refs[ng:]
    mixed, refs = (refs[0], refs[1:]) if extra else (None, refs)
    cos_held, sin_held, acc_even, acc_odd = refs[:4]
    rows = ahead[0].shape[0]
    kept = channels.shape[1]
    step = pl.program_id(0)
    low = [p for p, (_, wanted) in enumerate(planes) if wanted]
    place = {p: (len(planes) + i) * rows for i, p in enumerate(low)}
    width = 2 * LANES
    span = DEPTH * PER_STEP
    backwards = LANES - 1 - lax.broadcasted_iota(jnp.int32, (CHUNK, LANES), 1)

    @pl.when(step == 0)
    def _():
        fill_angles(channels, cos_held, sin_held)
        acc_even[...] = jnp.zeros_like(acc_even)
        acc_odd[...] = jnp.zeros_like(acc_odd)

    for u in range(PER_STEP):
        even, odd, t_even, t_odd = refs[4 + 4 * u : 8 + 4 * u]
        for b in range(DEPTH // SUB):
            start = SUB + step * (span // SUB) + u * (DEPTH // SUB) + b
            for q in range(0, SUB, CHUNK):
                here = slice(b * SUB + q, b * SUB + q + CHUNK)
                cos_b, sin_b = cos_held[pl.ds(start, 1), :], sin_held[pl.ds(start, 1), :]
                cos_q, sin_q = cos_held[q : q + CHUNK, :], sin_held[q : q + CHUNK, :]
                for held, table in (
                    (t_even, cos_b * cos_q - sin_b * sin_q),
                    (t_odd, sin_b * cos_q + cos_b * sin_q),
                ):
                    high = table.astype(jnp.bfloat16)
                    held[here, :kept] = high
                    held[here, kept:] = (table - high.astype(jnp.float32)).astype(jnp.bfloat16)
        for w in range(0, DEPTH, width):
            at = u * DEPTH + w
            taps = [jnp.broadcast_to(coeff[t : t + 1, at : at + width], (CHUNK, width)) for t in range(TAPS)]
            for r in range(0, rows, CHUNK):
                fore, rear = {}, {}
                for i, f in enumerate(frames):
                    fore[f] = ahead[i][r : r + CHUNK, at : at + width].astype(jnp.float32)
                    seen = mirror[i][r : r + CHUNK, span - at - width : span - at].astype(jnp.float32)
                    rear[f] = jnp.concatenate(
                        [
                            jnp.take_along_axis(seen[:, c : c + LANES], backwards, axis=1)
                            for c in range(width - LANES, -1, -LANES)
                        ],
                        axis=1,
                    )
                for p, (s, _) in enumerate(planes):
                    x = z = None
                    for t in range(TAPS):
                        f = s - (TAPS - 1) + t
                        if f in fore:
                            a, b = taps[t] * fore[f], taps[TAPS - 1 - t] * rear[f]
                            x, z = (a, b) if x is None else (x + a, z + b)
                    for value, held in ((x + z, even), (x - z, odd)):
                        high = value.astype(jnp.bfloat16)
                        held[p * rows + r : p * rows + r + CHUNK, w : w + width] = high
                        if p in place:
                            rest = (value - high.astype(jnp.float32)).astype(jnp.bfloat16)
                            held[place[p] + r : place[p] + r + CHUNK, w : w + width] = rest
        acc_even[...] += jnp.dot(even[...], t_even[...], preferred_element_type=jnp.float32)
        acc_odd[...] += jnp.dot(odd[...], t_odd[...], preferred_element_type=jnp.float32)

    @pl.when(step == pl.num_programs(0) - 1)
    def _():
        def total(acc, p):
            value = acc[p * rows : (p + 1) * rows, :kept] + acc[p * rows : (p + 1) * rows, kept:]
            if p in place:
                rest = slice(place[p], place[p] + rows)
                value = value + acc[rest, :kept] + acc[rest, kept:]
            return value

        cos_h, sin_h = cos_held[0:1, :], sin_held[0:1, :]
        scale = codes[...].astype(jnp.float32) * (TRANSFORM**-0.5 / 16.0)
        def spectrum(p):
            even, odd = total(acc_even, p), total(acc_odd, p)
            return (cos_h * even + sin_h * odd).T * scale, (sin_h * even - cos_h * odd).T * scale

        if extra:
            mix([spectrum(p) for p in groups[0][0]], parts, *arrived[:3], outs[0], mixed)
        else:
            for out, (members, dtype) in zip(outs, groups):
                for i, p in enumerate(members):
                    out[i, :kept], out[i, kept:] = (v.astype(dtype) for v in spectrum(p))


def edge_kernel(planes, frames, groups, *refs):
    nf, ng = len(frames), len(groups)
    volts, (coeff, channels, codes) = refs[:nf], refs[nf : nf + 3]
    outs, (cos_held, sin_held, acc, *held) = refs[nf + 3 : nf + 3 + ng], refs[nf + 3 + ng :]
    rows, span = volts[0].shape
    kept = channels.shape[1]
    step = pl.program_id(0)
    width = 2 * LANES

    @pl.when(step == 0)
    def _():
        fill_angles(channels, cos_held, sin_held, 0)
        acc[...] = jnp.zeros_like(acc)

    for u in range(span // EDGE_DEPTH):
        filtered, table = held[2 * u : 2 * u + 2]
        for b in range(EDGE_DEPTH // SUB):
            start = SUB + step * (span // SUB) + u * (EDGE_DEPTH // SUB) + b
            for q in range(0, SUB, CHUNK):
                here = slice(b * SUB + q, b * SUB + q + CHUNK)
                cos_b, sin_b = cos_held[pl.ds(start, 1), :], sin_held[pl.ds(start, 1), :]
                cos_q, sin_q = cos_held[q : q + CHUNK, :], sin_held[q : q + CHUNK, :]
                table[here, :kept] = (cos_b * cos_q - sin_b * sin_q).astype(jnp.bfloat16)
                table[here, kept:] = (-sin_b * cos_q - cos_b * sin_q).astype(jnp.bfloat16)
        for w in range(0, EDGE_DEPTH, width):
            at = u * EDGE_DEPTH + w
            taps = [jnp.broadcast_to(coeff[t : t + 1, at : at + width], (CHUNK, width)) for t in range(TAPS)]
            for r in range(0, rows, CHUNK):
                seen = {
                    f: volts[i][r : r + CHUNK, at : at + width].astype(jnp.float32) for i, f in enumerate(frames)
                }
                for p, s in enumerate(planes):
                    terms = [taps[t] * seen[s - (TAPS - 1) + t] for t in range(TAPS) if s - (TAPS - 1) + t in seen]
                    filtered[p * rows + r : p * rows + r + CHUNK, w : w + width] = sum(terms[1:], terms[0]).astype(
                        jnp.bfloat16
                    )
        acc[...] += jnp.dot(filtered[...], table[...], preferred_element_type=jnp.float32)

    @pl.when(step == pl.num_programs(0) - 1)
    def _():
        scale = codes[...].astype(jnp.float32) * (TRANSFORM**-0.5 / 16.0)
        for out, members in zip(outs, groups):
            for i, p in enumerate(members):
                out[i] = (acc[p * rows : (p + 1) * rows, :].T * scale).astype(out.dtype)


def edges(voltages, coeffs, channels, codes, planes, groups):
    rows = voltages.shape[0]
    own = voltages.shape[1] // TRANSFORM
    kept = channels.shape[1]
    span = EDGE_DEPTH * EDGE_STEPS
    steps = TRANSFORM // span
    frames = sorted({s - (TAPS - 1) + t for s in planes for t in range(TAPS)} & set(range(own)))

    def frame(f):
        return pl.BlockSpec((rows, span), lambda j: (0, f * steps + j))

    outs = [jax.ShapeDtypeStruct((len(m), 2 * kept, rows), jnp.bfloat16) for m in groups]
    table = pltpu.VMEM((SUB + TRANSFORM // SUB, kept), jnp.float32)
    return pl.pallas_call(
        functools.partial(edge_kernel, planes, frames, groups),
        grid=(steps,),
        in_specs=[frame(f) for f in frames]
        + [pl.BlockSpec((TAPS, span), lambda j: (0, j)), pl.BlockSpec((1, kept), lambda j: (0, 0))]
        + [pl.BlockSpec((1, rows), lambda j: (0, 0))],
        out_specs=[pl.BlockSpec(o.shape, lambda j: (0, 0, 0)) for o in outs],
        out_shape=outs,
        scratch_shapes=[table, table, pltpu.VMEM((len(planes) * rows, 2 * kept), jnp.float32)]
        + [
            pltpu.VMEM((len(planes) * rows, EDGE_DEPTH), jnp.bfloat16),
            pltpu.VMEM((EDGE_DEPTH, 2 * kept), jnp.bfloat16),
        ]
        * EDGE_STEPS,
        compiler_params=pltpu.CompilerParams(vmem_limit_bytes=VMEM),
        cost_estimate=pl.CostEstimate(
            flops=4 * rows * TRANSFORM * kept * len(planes),
            bytes_accessed=len(frames) * rows * TRANSFORM * 2,
            transcendentals=0,
        ),
    )(*[voltages] * len(frames), coeffs, channels, codes)


def spectra(voltages, coeffs, channels, codes, planes, groups, piece=0, pieces=1, arrived=(), parts=1):
    rows = voltages.shape[0] // pieces
    own = voltages.shape[1] // TRANSFORM
    span = DEPTH * PER_STEP
    steps = TRANSFORM // 2 // span
    kept = channels.shape[1]
    columns = 2 * kept
    frames = sorted({s - (TAPS - 1) + t for s, _ in planes for t in range(TAPS)} & set(range(own)))
    count = len(planes) + sum(wanted for _, wanted in planes)

    def ahead(f):
        return pl.BlockSpec((rows, span), lambda j: (piece, 2 * f * steps + j))

    def mirror(f):
        return pl.BlockSpec((rows, span), lambda j: (piece, 2 * f * steps + 2 * steps - 1 - j))

    if arrived:
        outs = [jax.ShapeDtypeStruct((parts, columns * len(planes) // parts, rows), jnp.bfloat16)]
        held = [pltpu.VMEM((rows // LANES, len(planes) * columns, LANES), jnp.float32)]
        came = [pl.BlockSpec(memory_space=pltpu.SMEM)] + [
            pl.BlockSpec((x.shape[0], columns, rows), lambda j: (0, 0, piece)) for x in arrived[1:3]
        ]
        came += [pl.BlockSpec(memory_space=pl.ANY)] * len(arrived[3:])
    else:
        outs = [jax.ShapeDtypeStruct((len(m), columns, rows), d) for m, d in groups]
        held, came = [], []
    table = pltpu.VMEM((SUB + TRANSFORM // 2 // SUB, kept), jnp.float32)
    part = [
        pltpu.VMEM((count * rows, DEPTH), jnp.bfloat16),
        pltpu.VMEM((count * rows, DEPTH), jnp.bfloat16),
        pltpu.VMEM((DEPTH, columns), jnp.bfloat16),
        pltpu.VMEM((DEPTH, columns), jnp.bfloat16),
    ]
    return pl.pallas_call(
        functools.partial(dft_kernel, planes, frames, groups, len(came), parts),
        grid=(steps,),
        in_specs=[ahead(f) for f in frames]
        + [mirror(f) for f in frames]
        + [pl.BlockSpec((TAPS, span), lambda j: (0, j)), pl.BlockSpec((1, kept), lambda j: (0, 0))]
        + [pl.BlockSpec((1, rows), lambda j: (0, piece)), *came],
        out_specs=[pl.BlockSpec(o.shape, lambda j: (0, 0, 0)) for o in outs],
        out_shape=outs,
        scratch_shapes=[*held, table, table]
        + [pltpu.VMEM((count * rows, columns), jnp.float32)] * 2
        + part * PER_STEP,
        compiler_params=pltpu.CompilerParams(vmem_limit_bytes=VMEM),
        cost_estimate=pl.CostEstimate(
            flops=2 * rows * TRANSFORM * columns * count,
            bytes_accessed=len(frames) * rows * TRANSFORM * 2,
            transcendentals=0,
        ),
    )(*[voltages] * (2 * len(frames)), coeffs, channels, codes, *arrived)


def combine_kernel(parts, place, own, ahead, behind, out, mixed):
    kept = own.shape[1] // 2
    mix([(own[s, :kept], own[s, kept:]) for s in range(own.shape[0])], parts, place, ahead, behind, out, mixed)


def combined(parts, me, own, ahead, behind, piece):
    slots, columns, rows = own.shape
    block = columns * slots // parts

    def arriving(x):
        return pl.BlockSpec((x.shape[0], columns, rows), lambda j: (0, 0, piece))

    return pl.pallas_call(
        functools.partial(combine_kernel, parts),
        grid=(1,),
        in_specs=[pl.BlockSpec(memory_space=pltpu.SMEM), pl.BlockSpec(own.shape, lambda j: (0, 0, 0))]
        + [arriving(ahead), arriving(behind)],
        out_specs=pl.BlockSpec((parts, block, rows), lambda j: (0, 0, 0)),
        out_shape=jax.ShapeDtypeStruct((parts, block, rows), jnp.bfloat16),
        scratch_shapes=[pltpu.VMEM((rows // LANES, slots * columns, LANES), jnp.float32)],
        compiler_params=pltpu.CompilerParams(vmem_limit_bytes=VMEM),
    )(me, own, ahead, behind)


def correlate_kernel(half, pair, spectra_count, pieces, sets, groups, seat, *refs):
    out, buffer, sems = refs[-3:]
    wide = 2 * half
    tile = 16 // wide
    me = seat[0]

    def copy(channel, slot):
        return pltpu.make_async_copy(buffer.at[slot], out.at[:, channel], sems.at[slot])

    def gathered(tiles, take):
        return jnp.concatenate([jnp.concatenate([t[take] for t in p], axis=0) for p in tiles], axis=1)

    def turn(step, carry):
        for group in range(pair // tile):
            at = pl.multiple_of((step * pair + group * tile) * wide, 16)
            tiles = [
                [
                    [
                        refs[(m * pieces + p) * sets + k][i, pl.ds(at, 16), :].astype(jnp.float32)
                        for k in range(sets)
                        for i in range(refs[k].shape[0])
                    ]
                    for p in range(pieces)
                ]
                for m in range(groups)
            ]
            for h in range(tile):
                c = group * tile + h
                columns = [gathered(t, slice(h * wide, (h + 1) * wide)) for t in tiles]
                left = columns[0]
                bit = 1
                while bit < groups:
                    swap = (me // bit) % 2 == 1
                    columns = [jnp.where(swap, columns[q ^ bit], columns[q]) for q in range(groups)]
                    bit *= 2
                right = jnp.concatenate(columns, axis=1).astype(jnp.bfloat16)
                row = lax.broadcasted_iota(jnp.int32, left.shape, 0) % wide
                turned = jnp.where(row < half, pltpu.roll(left, left.shape[0] - half, 0), -pltpu.roll(left, half, 0))
                both = jnp.concatenate([left.T, turned.T], axis=0).astype(jnp.bfloat16)
                result = jnp.dot(both, right, preferred_element_type=jnp.float32) * (1.0 / spectra_count)

                @pl.when(step > 0)
                def _():
                    copy(step * pair + c, c).wait()

                buffer[c, 0], buffer[c, 1] = result[: left.shape[1]], result[left.shape[1] :]
                copy(step * pair + c, c).start()
        return carry

    turns = out.shape[1] // pair
    lax.fori_loop(0, turns, turn, 0)
    for c in range(pair):
        copy((turns - 1) * pair + c, c).wait()


def correlated(seat, seen, half, spectra_count):
    groups, pieces, sets = len(seen), len(seen[0]), len(seen[0][0])
    wide = 2 * half
    block = seen[0][0][0].shape[1]
    rows = sum(p[0].shape[2] for p in seen[0])
    channels = block // wide
    pair = min(channels, 4)
    arrays = [a for mask in seen for piece in mask for a in piece]
    return pl.pallas_call(
        functools.partial(correlate_kernel, half, pair, spectra_count, pieces, sets, groups),
        grid_spec=pltpu.PrefetchScalarGridSpec(
            num_scalar_prefetch=1,
            grid=(1,),
            in_specs=[pl.BlockSpec(a.shape, lambda j, seat: (0, 0, 0)) for a in arrays],
            out_specs=pl.BlockSpec(memory_space=pl.ANY),
            scratch_shapes=[
                pltpu.VMEM((pair, 2, rows, groups * rows), jnp.float32),
                pltpu.SemaphoreType.DMA((pair,)),
            ],
        ),
        out_shape=jax.ShapeDtypeStruct((2, channels, rows, groups * rows), jnp.float32),
        compiler_params=pltpu.CompilerParams(vmem_limit_bytes=VMEM),
        cost_estimate=pl.CostEstimate(
            flops=8 * spectra_count * rows * groups * rows * channels,
            bytes_accessed=2 * channels * rows * groups * rows * 4,
            transcendentals=0,
        ),
    )(seat, *arrays)


def exchanged(block, axis, mask):
    return lax.ppermute(block, axis, [(i, i ^ mask) for i in range(lax.axis_size(axis))])


def local(voltages, scale_codes, kept_channels):
    rows = voltages.shape[0]
    own = voltages.shape[1] // TRANSFORM
    history = TAPS - 1
    parts, groups = lax.axis_size("chan"), lax.axis_size("inp")
    me, seat = lax.axis_index("chan"), lax.axis_index("inp")
    coeffs = prototype()
    channels = kept_channels[None, :]
    codes = scale_codes[None, :]
    first = 2
    last = first + own
    edge = [*range(first), *range(last, own + history)]
    inner = [(s, s < last - 1) for s in range(first, last)]
    behind, ahead = edges(
        voltages, coeffs, channels, codes, edge, [list(range(first)), list(range(first, len(edge)))]
    )
    ahead = lax.ppermute(ahead, "chan", [(i, i + 1) for i in range(parts - 1)])
    behind = lax.ppermute(behind, "chan", [(i, (i - 1) % parts) for i in range(parts)])
    me, seat = me.astype(jnp.int32).reshape(1), seat.astype(jnp.int32).reshape(1)
    mine = []
    whole = [(list(range(own)), jnp.float32)]
    for piece in range(PIECES):
        if piece == 0:
            (planes,) = spectra(voltages, coeffs, channels, codes, inner, whole, piece, PIECES)
            blocks = combined(parts, me, planes, ahead, behind, piece)
        else:
            (blocks,) = spectra(
                voltages, coeffs, channels, codes, inner, whole, piece, PIECES, (me, ahead, behind, blocks), parts
            )
        mine.append([lax.all_to_all(blocks, "chan", 0, 0, tiled=True)])
    seen = {0: mine}
    bit = groups // 2
    while bit:
        seen.update({m | bit: [[exchanged(b, "inp", bit) for b in p] for p in seen[m]] for m in list(seen)})
        bit //= 2
    return correlated(seat, [seen[m] for m in range(groups)], own, own * parts)


def solution(mesh):
    placed = (P("inp", "chan"), P("inp"), P())
    return jax.shard_map(
        local, mesh=mesh, in_specs=placed, out_specs=P(None, "chan", "inp", None), check_vma=False
    )
```

```python
import functools

import jax
import jax.numpy as jnp
import numpy as np
from jax import lax
from jax.experimental import pallas as pl
from jax.experimental.pallas import tpu as pltpu
from jax.sharding import PartitionSpec as P

TRANSFORM = 8192
TAPS = 4
LANES = 128
SUB = 128
DEPTH = 512
PER_STEP = 2
CHUNK = 16
EDGE_CHUNK = 32
EDGE_DEPTH = 1024
EDGE_STEPS = 2
VMEM = 60 * 1024 * 1024
PIECES = 2


def prototype():
    sample = np.arange(TAPS * TRANSFORM, dtype=np.float64).reshape(TAPS, TRANSFORM)
    offset = (sample + 0.5) / TRANSFORM - TAPS / 2.0
    window = 0.5 - 0.5 * np.cos(2.0 * np.pi * (sample + 0.5) / (TAPS * TRANSFORM))
    return (np.sinc(offset) * window).astype(np.float32)


def fill_angles(kept, cos_held, sin_held, half=1):
    circle = 2 * TRANSFORM
    row = lax.broadcasted_iota(jnp.int32, cos_held.shape, 0)
    twice = jnp.where(row < SUB, 2 * row + half, 2 * SUB * (row - SUB))
    turns = jnp.bitwise_and(kept[...] * twice, circle - 1)
    angles = turns.astype(jnp.float32) * (2.0 * np.pi / circle)
    cos_held[...] = jnp.cos(angles)
    sin_held[...] = jnp.sin(angles)


def mix(spectra, parts, place, ahead, behind, out, mixed):
    slots, kept = len(spectra), spectra[0][0].shape[0]
    inside = jnp.where(place[0] == parts - 1, 0.0, 1.0)
    back = behind.shape[0]
    for s, values in enumerate(spectra):
        for p, value in enumerate(values):
            here = slice(p * kept, (p + 1) * kept)
            if s == 0:
                value = value + ahead[0, here].astype(jnp.float32)
            if s >= slots - back:
                value = value * inside + behind[s - (slots - back), here].astype(jnp.float32)
            for h in range(mixed.shape[0]):
                mixed[h, pl.ds(p * slots + s, kept, stride=2 * slots), :] = value[:, h * LANES : (h + 1) * LANES]
    rows = out.shape[1]
    for h in range(mixed.shape[0]):
        for i in range(out.shape[0]):
            out[i, :, h * LANES : (h + 1) * LANES] = mixed[h, i * rows : (i + 1) * rows, :].astype(out.dtype)


def dft_kernel(planes, frames, groups, extra, parts, *refs):
    nf, ng = len(frames), len(groups)
    ahead, mirror = refs[:nf], refs[nf : 2 * nf]
    coeff, channels, codes = refs[2 * nf : 2 * nf + 3]
    arrived, refs = refs[2 * nf + 3 : 2 * nf + 3 + extra], refs[2 * nf + 3 + extra :]
    outs, refs = refs[:ng], refs[ng:]
    mixed, refs = (refs[0], refs[1:]) if extra else (None, refs)
    cos_held, sin_held, acc_even, acc_odd = refs[:4]
    rows = ahead[0].shape[0]
    kept = channels.shape[1]
    step = pl.program_id(0)
    low = [p for p, (_, wanted) in enumerate(planes) if wanted]
    place = {p: (len(planes) + i) * rows for i, p in enumerate(low)}
    width = 4 * LANES
    span = DEPTH * PER_STEP
    backwards = LANES - 1 - lax.broadcasted_iota(jnp.int32, (CHUNK, LANES), 1)

    @pl.when(step == 0)
    def _():
        fill_angles(channels, cos_held, sin_held)
        acc_even[...] = jnp.zeros_like(acc_even)
        acc_odd[...] = jnp.zeros_like(acc_odd)

    for u in range(PER_STEP):
        even, odd, t_even, t_odd = refs[4 + 4 * u : 8 + 4 * u]
        for b in range(DEPTH // SUB):
            start = SUB + step * (span // SUB) + u * (DEPTH // SUB) + b
            for q in range(0, SUB, CHUNK):
                here = slice(b * SUB + q, b * SUB + q + CHUNK)
                cos_b, sin_b = cos_held[pl.ds(start, 1), :], sin_held[pl.ds(start, 1), :]
                cos_q, sin_q = cos_held[q : q + CHUNK, :], sin_held[q : q + CHUNK, :]
                for held, table in (
                    (t_even, cos_b * cos_q - sin_b * sin_q),
                    (t_odd, sin_b * cos_q + cos_b * sin_q),
                ):
                    high = table.astype(jnp.bfloat16)
                    held[here, :kept] = high
                    held[here, kept:] = (table - high.astype(jnp.float32)).astype(jnp.bfloat16)
        for w in range(0, DEPTH, width):
            at = u * DEPTH + w
            taps = [jnp.broadcast_to(coeff[t : t + 1, at : at + width], (CHUNK, width)) for t in range(TAPS)]
            for r in range(0, rows, CHUNK):
                fore, rear = {}, {}
                for i, f in enumerate(frames):
                    fore[f] = ahead[i][r : r + CHUNK, at : at + width].astype(jnp.float32)
                    seen = mirror[i][r : r + CHUNK, span - at - width : span - at].astype(jnp.float32)
                    rear[f] = jnp.concatenate(
                        [
                            jnp.take_along_axis(seen[:, c : c + LANES], backwards, axis=1)
                            for c in range(width - LANES, -1, -LANES)
                        ],
                        axis=1,
                    )
                for p, (s, _) in enumerate(planes):
                    x = z = None
                    for t in range(TAPS):
                        f = s - (TAPS - 1) + t
                        if f in fore:
                            a, b = taps[t] * fore[f], taps[TAPS - 1 - t] * rear[f]
                            x, z = (a, b) if x is None else (x + a, z + b)
                    for value, held in ((x + z, even), (x - z, odd)):
                        high = value.astype(jnp.bfloat16)
                        held[p * rows + r : p * rows + r + CHUNK, w : w + width] = high
                        if p in place:
                            rest = (value - high.astype(jnp.float32)).astype(jnp.bfloat16)
                            held[place[p] + r : place[p] + r + CHUNK, w : w + width] = rest
        acc_even[...] += jnp.dot(even[...], t_even[...], preferred_element_type=jnp.float32)
        acc_odd[...] += jnp.dot(odd[...], t_odd[...], preferred_element_type=jnp.float32)

    @pl.when(step == pl.num_programs(0) - 1)
    def _():
        def total(acc, p):
            value = acc[p * rows : (p + 1) * rows, :kept] + acc[p * rows : (p + 1) * rows, kept:]
            if p in place:
                rest = slice(place[p], place[p] + rows)
                value = value + acc[rest, :kept] + acc[rest, kept:]
            return value

        cos_h, sin_h = cos_held[0:1, :], sin_held[0:1, :]
        scale = codes[...].astype(jnp.float32) * (TRANSFORM**-0.5 / 16.0)
        def spectrum(p):
            even, odd = total(acc_even, p), total(acc_odd, p)
            return (cos_h * even + sin_h * odd).T * scale, (sin_h * even - cos_h * odd).T * scale

        if extra:
            mix([spectrum(p) for p in groups[0][0]], parts, *arrived[:3], outs[0], mixed)
        else:
            for out, (members, dtype) in zip(outs, groups):
                for i, p in enumerate(members):
                    out[i, :kept], out[i, kept:] = (v.astype(dtype) for v in spectrum(p))


def edge_kernel(planes, frames, groups, *refs):
    nf, ng = len(frames), len(groups)
    volts, (coeff, channels, codes) = refs[:nf], refs[nf : nf + 3]
    outs, (cos_held, sin_held, acc, *held) = refs[nf + 3 : nf + 3 + ng], refs[nf + 3 + ng :]
    rows, span = volts[0].shape
    kept = channels.shape[1]
    step = pl.program_id(0)
    width = 2 * LANES

    @pl.when(step == 0)
    def _():
        fill_angles(channels, cos_held, sin_held, 0)
        acc[...] = jnp.zeros_like(acc)

    for u in range(span // EDGE_DEPTH):
        filtered, table = held[2 * u : 2 * u + 2]
        for b in range(EDGE_DEPTH // SUB):
            start = SUB + step * (span // SUB) + u * (EDGE_DEPTH // SUB) + b
            for q in range(0, SUB, EDGE_CHUNK):
                here = slice(b * SUB + q, b * SUB + q + EDGE_CHUNK)
                cos_b, sin_b = cos_held[pl.ds(start, 1), :], sin_held[pl.ds(start, 1), :]
                cos_q, sin_q = cos_held[q : q + EDGE_CHUNK, :], sin_held[q : q + EDGE_CHUNK, :]
                table[here, :kept] = (cos_b * cos_q - sin_b * sin_q).astype(jnp.bfloat16)
                table[here, kept:] = (-sin_b * cos_q - cos_b * sin_q).astype(jnp.bfloat16)
        for w in range(0, EDGE_DEPTH, width):
            at = u * EDGE_DEPTH + w
            taps = [jnp.broadcast_to(coeff[t : t + 1, at : at + width], (EDGE_CHUNK, width)) for t in range(TAPS)]
            for r in range(0, rows, EDGE_CHUNK):
                seen = {
                    f: volts[i][r : r + EDGE_CHUNK, at : at + width].astype(jnp.float32) for i, f in enumerate(frames)
                }
                for p, s in enumerate(planes):
                    terms = [taps[t] * seen[s - (TAPS - 1) + t] for t in range(TAPS) if s - (TAPS - 1) + t in seen]
                    filtered[p * rows + r : p * rows + r + EDGE_CHUNK, w : w + width] = sum(terms[1:], terms[0]).astype(
                        jnp.bfloat16
                    )
        acc[...] += jnp.dot(filtered[...], table[...], preferred_element_type=jnp.float32)

    @pl.when(step == pl.num_programs(0) - 1)
    def _():
        scale = codes[...].astype(jnp.float32) * (TRANSFORM**-0.5 / 16.0)
        for out, members in zip(outs, groups):
            for i, p in enumerate(members):
                out[i] = (acc[p * rows : (p + 1) * rows, :].T * scale).astype(out.dtype)


def edges(voltages, coeffs, channels, codes, planes, groups):
    rows = voltages.shape[0]
    own = voltages.shape[1] // TRANSFORM
    kept = channels.shape[1]
    span = EDGE_DEPTH * EDGE_STEPS
    steps = TRANSFORM // span
    frames = sorted({s - (TAPS - 1) + t for s in planes for t in range(TAPS)} & set(range(own)))

    def frame(f):
        return pl.BlockSpec((rows, span), lambda j: (0, f * steps + j))

    outs = [jax.ShapeDtypeStruct((len(m), 2 * kept, rows), jnp.bfloat16) for m in groups]
    table = pltpu.VMEM((SUB + TRANSFORM // SUB, kept), jnp.float32)
    return pl.pallas_call(
        functools.partial(edge_kernel, planes, frames, groups),
        grid=(steps,),
        in_specs=[frame(f) for f in frames]
        + [pl.BlockSpec((TAPS, span), lambda j: (0, j)), pl.BlockSpec((1, kept), lambda j: (0, 0))]
        + [pl.BlockSpec((1, rows), lambda j: (0, 0))],
        out_specs=[pl.BlockSpec(o.shape, lambda j: (0, 0, 0)) for o in outs],
        out_shape=outs,
        scratch_shapes=[table, table, pltpu.VMEM((len(planes) * rows, 2 * kept), jnp.float32)]
        + [
            pltpu.VMEM((len(planes) * rows, EDGE_DEPTH), jnp.bfloat16),
            pltpu.VMEM((EDGE_DEPTH, 2 * kept), jnp.bfloat16),
        ]
        * EDGE_STEPS,
        compiler_params=pltpu.CompilerParams(vmem_limit_bytes=VMEM),
        cost_estimate=pl.CostEstimate(
            flops=4 * rows * TRANSFORM * kept * len(planes),
            bytes_accessed=len(frames) * rows * TRANSFORM * 2,
            transcendentals=0,
        ),
    )(*[voltages] * len(frames), coeffs, channels, codes)


def spectra(voltages, coeffs, channels, codes, planes, groups, piece=0, pieces=1, arrived=(), parts=1):
    rows = voltages.shape[0] // pieces
    own = voltages.shape[1] // TRANSFORM
    span = DEPTH * PER_STEP
    steps = TRANSFORM // 2 // span
    kept = channels.shape[1]
    columns = 2 * kept
    frames = sorted({s - (TAPS - 1) + t for s, _ in planes for t in range(TAPS)} & set(range(own)))
    count = len(planes) + sum(wanted for _, wanted in planes)

    def ahead(f):
        return pl.BlockSpec((rows, span), lambda j: (piece, 2 * f * steps + j))

    def mirror(f):
        return pl.BlockSpec((rows, span), lambda j: (piece, 2 * f * steps + 2 * steps - 1 - j))

    if arrived:
        outs = [jax.ShapeDtypeStruct((parts, columns * len(planes) // parts, rows), jnp.bfloat16)]
        held = [pltpu.VMEM((rows // LANES, len(planes) * columns, LANES), jnp.float32)]
        came = [pl.BlockSpec(memory_space=pltpu.SMEM)] + [
            pl.BlockSpec((x.shape[0], columns, rows), lambda j: (0, 0, piece)) for x in arrived[1:3]
        ]
        came += [pl.BlockSpec(memory_space=pl.ANY)] * len(arrived[3:])
    else:
        outs = [jax.ShapeDtypeStruct((len(m), columns, rows), d) for m, d in groups]
        held, came = [], []
    table = pltpu.VMEM((SUB + TRANSFORM // 2 // SUB, kept), jnp.float32)
    part = [
        pltpu.VMEM((count * rows, DEPTH), jnp.bfloat16),
        pltpu.VMEM((count * rows, DEPTH), jnp.bfloat16),
        pltpu.VMEM((DEPTH, columns), jnp.bfloat16),
        pltpu.VMEM((DEPTH, columns), jnp.bfloat16),
    ]
    return pl.pallas_call(
        functools.partial(dft_kernel, planes, frames, groups, len(came), parts),
        grid=(steps,),
        in_specs=[ahead(f) for f in frames]
        + [mirror(f) for f in frames]
        + [pl.BlockSpec((TAPS, span), lambda j: (0, j)), pl.BlockSpec((1, kept), lambda j: (0, 0))]
        + [pl.BlockSpec((1, rows), lambda j: (0, piece)), *came],
        out_specs=[pl.BlockSpec(o.shape, lambda j: (0, 0, 0)) for o in outs],
        out_shape=outs,
        scratch_shapes=[*held, table, table]
        + [pltpu.VMEM((count * rows, columns), jnp.float32)] * 2
        + part * PER_STEP,
        compiler_params=pltpu.CompilerParams(vmem_limit_bytes=VMEM),
        cost_estimate=pl.CostEstimate(
            flops=2 * rows * TRANSFORM * columns * count,
            bytes_accessed=len(frames) * rows * TRANSFORM * 2,
            transcendentals=0,
        ),
    )(*[voltages] * (2 * len(frames)), coeffs, channels, codes, *arrived)


def combine_kernel(parts, place, own, ahead, behind, out, mixed):
    kept = own.shape[1] // 2
    mix([(own[s, :kept], own[s, kept:]) for s in range(own.shape[0])], parts, place, ahead, behind, out, mixed)


def combined(parts, me, own, ahead, behind, piece):
    slots, columns, rows = own.shape
    block = columns * slots // parts

    def arriving(x):
        return pl.BlockSpec((x.shape[0], columns, rows), lambda j: (0, 0, piece))

    return pl.pallas_call(
        functools.partial(combine_kernel, parts),
        grid=(1,),
        in_specs=[pl.BlockSpec(memory_space=pltpu.SMEM), pl.BlockSpec(own.shape, lambda j: (0, 0, 0))]
        + [arriving(ahead), arriving(behind)],
        out_specs=pl.BlockSpec((parts, block, rows), lambda j: (0, 0, 0)),
        out_shape=jax.ShapeDtypeStruct((parts, block, rows), jnp.bfloat16),
        scratch_shapes=[pltpu.VMEM((rows // LANES, slots * columns, LANES), jnp.float32)],
        compiler_params=pltpu.CompilerParams(vmem_limit_bytes=VMEM),
    )(me, own, ahead, behind)


def correlate_kernel(half, pair, spectra_count, pieces, sets, groups, seat, *refs):
    out, buffer, sems = refs[-3:]
    wide = 2 * half
    tile = 16 // wide
    me = seat[0]

    def copy(channel, slot):
        return pltpu.make_async_copy(buffer.at[slot], out.at[:, channel], sems.at[slot])

    def gathered(tiles, take):
        return jnp.concatenate([jnp.concatenate([t[take] for t in p], axis=0) for p in tiles], axis=1)

    def turn(step, carry):
        for group in range(pair // tile):
            at = pl.multiple_of((step * pair + group * tile) * wide, 16)
            tiles = [
                [
                    [
                        refs[(m * pieces + p) * sets + k][i, pl.ds(at, 16), :].astype(jnp.float32)
                        for k in range(sets)
                        for i in range(refs[k].shape[0])
                    ]
                    for p in range(pieces)
                ]
                for m in range(groups)
            ]
            for h in range(tile):
                c = group * tile + h
                columns = [gathered(t, slice(h * wide, (h + 1) * wide)) for t in tiles]
                left = columns[0]
                bit = 1
                while bit < groups:
                    swap = (me // bit) % 2 == 1
                    columns = [jnp.where(swap, columns[q ^ bit], columns[q]) for q in range(groups)]
                    bit *= 2
                right = jnp.concatenate(columns, axis=1).astype(jnp.bfloat16)
                row = lax.broadcasted_iota(jnp.int32, left.shape, 0) % wide
                turned = jnp.where(row < half, pltpu.roll(left, left.shape[0] - half, 0), -pltpu.roll(left, half, 0))
                both = jnp.concatenate([left.T, turned.T], axis=0).astype(jnp.bfloat16)
                result = jnp.dot(both, right, preferred_element_type=jnp.float32) * (1.0 / spectra_count)

                @pl.when(step > 0)
                def _():
                    copy(step * pair + c, c).wait()

                buffer[c, 0], buffer[c, 1] = result[: left.shape[1]], result[left.shape[1] :]
                copy(step * pair + c, c).start()
        return carry

    turns = out.shape[1] // pair
    lax.fori_loop(0, turns, turn, 0)
    for c in range(pair):
        copy((turns - 1) * pair + c, c).wait()


def correlated(seat, seen, half, spectra_count):
    groups, pieces, sets = len(seen), len(seen[0]), len(seen[0][0])
    wide = 2 * half
    block = seen[0][0][0].shape[1]
    rows = sum(p[0].shape[2] for p in seen[0])
    channels = block // wide
    pair = min(channels, 4)
    arrays = [a for mask in seen for piece in mask for a in piece]
    return pl.pallas_call(
        functools.partial(correlate_kernel, half, pair, spectra_count, pieces, sets, groups),
        grid_spec=pltpu.PrefetchScalarGridSpec(
            num_scalar_prefetch=1,
            grid=(1,),
            in_specs=[pl.BlockSpec(a.shape, lambda j, seat: (0, 0, 0)) for a in arrays],
            out_specs=pl.BlockSpec(memory_space=pl.ANY),
            scratch_shapes=[
                pltpu.VMEM((pair, 2, rows, groups * rows), jnp.float32),
                pltpu.SemaphoreType.DMA((pair,)),
            ],
        ),
        out_shape=jax.ShapeDtypeStruct((2, channels, rows, groups * rows), jnp.float32),
        compiler_params=pltpu.CompilerParams(vmem_limit_bytes=VMEM),
        cost_estimate=pl.CostEstimate(
            flops=8 * spectra_count * rows * groups * rows * channels,
            bytes_accessed=2 * channels * rows * groups * rows * 4,
            transcendentals=0,
        ),
    )(seat, *arrays)


def exchanged(block, axis, mask):
    return lax.ppermute(block, axis, [(i, i ^ mask) for i in range(lax.axis_size(axis))])


def local(voltages, scale_codes, kept_channels):
    rows = voltages.shape[0]
    own = voltages.shape[1] // TRANSFORM
    history = TAPS - 1
    parts, groups = lax.axis_size("chan"), lax.axis_size("inp")
    me, seat = lax.axis_index("chan"), lax.axis_index("inp")
    coeffs = prototype()
    channels = kept_channels[None, :]
    codes = scale_codes[None, :]
    first = 2
    last = first + own
    edge = [*range(first), *range(last, own + history)]
    inner = [(s, s < last - 1) for s in range(first, last)]
    behind, ahead = edges(
        voltages, coeffs, channels, codes, edge, [list(range(first)), list(range(first, len(edge)))]
    )
    ahead = lax.ppermute(ahead, "chan", [(i, i + 1) for i in range(parts - 1)])
    behind = lax.ppermute(behind, "chan", [(i, (i - 1) % parts) for i in range(parts)])
    me, seat = me.astype(jnp.int32).reshape(1), seat.astype(jnp.int32).reshape(1)
    mine = []
    whole = [(list(range(own)), jnp.float32)]
    for piece in range(PIECES):
        if piece == 0:
            (planes,) = spectra(voltages, coeffs, channels, codes, inner, whole, piece, PIECES)
            blocks = combined(parts, me, planes, ahead, behind, piece)
        else:
            (blocks,) = spectra(
                voltages, coeffs, channels, codes, inner, whole, piece, PIECES, (me, ahead, behind, blocks), parts
            )
        mine.append([lax.all_to_all(blocks, "chan", 0, 0, tiled=True)])
    seen = {0: mine}
    bit = groups // 2
    while bit:
        seen.update({m | bit: [[exchanged(b, "inp", bit) for b in p] for p in seen[m]] for m in list(seen)})
        bit //= 2
    return correlated(seat, [seen[m] for m in range(groups)], own, own * parts)


def solution(mesh):
    placed = (P("inp", "chan"), P("inp"), P())
    return jax.shard_map(
        local, mesh=mesh, in_specs=placed, out_specs=P(None, "chan", "inp", None), check_vma=False
    )
```
